32 devices in a mesh: row: 4 (over y, core), col: 8 (over z, x).
Axes of the slice: x: 2, y: 2, z: 4, core: 2. Of those that a mesh axis runs over, the one named last changes fastest.
Arguments:
- features: bfloat16 [4096, 128], P(('row', 'col')), may hold values from -6 to 6
- norm_weight: float32 [4096], P(('row', 'col')), may hold values from 0.01767767 to 0.110485435
- weight_in: bfloat16 [128, 256], replicated, may hold values from -6 to 6
- weight_out: bfloat16 [256, 128], replicated, may hold values from -6 to 6
- labels: int32 [4096], P(('row', 'col')), may hold values from 0 to 127
- tile_slot: int32 [32, 128], P(('row', 'col')), may hold values from 0 to 31
- tile_edges: int32 [32, 128, 2, 512], P(('row', 'col')), may hold values from 0 to 127
- tile_count: int32 [32], P(('row', 'col')), may hold values from 32 to 128, as said below
Outputs:
- grad_in: float32 [128, 256], replicated
- grad_out: float32 [256, 128], replicated
- loss: float32 [], replicated
The draws below stay inside these ranges and needn't reach their ends.
Inputs may be any that keep to these rules, and one draw needn't show every extreme that they name: `tile_slot`: position p of a slot covers the tile whose target rows start at 128 * (p // 4) and whose source columns start at 128 * (p % 4) within the device's block; a position may occur in several slots. Entry k of a slot marks row tile_edges[s, 0, k] and column tile_edges[s, 1, k] of its slot's tile; repeated entries count again. `tile_count`: slots at and after this number are not live; in every draw some device has all 128 slots live and another device only 32.
All inputs are finite; a program needn't handle non-finite values.
Results may differ from the reference program's by a relative error of at most 0.0084.
Values may be sent and summed in bfloat16 or wider, within the bound.
A program may use at most 64 MiB of HBM per device.

```python
import math
import jax
import jax.numpy as jnp
from jax import lax

IN = 128
HID = 256
CLS = 128
TILE = 128
EPT = 512
NODE_DEV = 128
TILES = 128
NODES = 4096
POSITIONS = 32
DEG = 512
N_ROW = 4
N_COL = 8
DEVICES = 32


def draw_tile_count(key, part):
    base_key = jax.random.fold_in(key, 11)
    first_key, second_key, third_key = jax.random.split(base_key, 3)
    counts = jax.random.randint(first_key, (DEVICES,), TILES // 4, TILES + 1)
    busiest = jax.random.randint(second_key, (), 0, DEVICES)
    lightest = (busiest + 1 + jax.random.randint(third_key, (), 0, DEVICES - 1)) % DEVICES
    counts = counts.at[busiest].set(TILES)
    counts = counts.at[lightest].set(TILES // 4)
    return counts.astype(jnp.int32)


def set_ends(array, own_key, low, high):
    longest = array.shape.index(max(array.shape))
    spots = []
    for shift in (0, 1):
        where = [jax.random.randint(jax.random.fold_in(own_key, axis), (), 0, length) for axis, length in enumerate(array.shape)]
        where[longest] = (where[longest] + shift) % array.shape[longest]
        spots.append(tuple(where))
    return array.at[spots[0]].set(low).at[spots[1]].set(high)


def block_levels(stream_key, extent, cuts, least, high):
    gain = 1.0
    for axis_at, shards_of in cuts:
        steps = jax.random.uniform(jax.random.fold_in(jax.random.fold_in(stream_key, 6), axis_at), (shards_of,), jnp.float32, least / len(cuts), high / len(cuts))
        gain = gain * jnp.repeat(jnp.exp(steps), extent[axis_at] // shards_of).reshape((-1,) + (1,) * (len(extent) - 1 - axis_at))
    return gain


def noise(rng, dims, deviation, most, cuts=(), held_as=jnp.bfloat16):
    values = jax.random.normal(rng, dims, jnp.float32) * deviation
    if len(cuts) > 0:
        values = block_levels(rng, dims, cuts, -0.22, 0.18) * values
    return jnp.clip(values, min=-most, max=most).astype(held_as)


def setup_inputs(seed: int = 0) -> dict:
    streams_of = jax.random.split(jax.random.key(seed), 9)
    features = noise(streams_of[0], (NODES, IN), 1.0, 6.0, ((0, 32),))
    norm_weight = jnp.clip(jnp.exp(math.log(0.110485435) - 1.8325814 * jax.random.uniform(streams_of[1], (NODES,), jnp.float32) ** block_levels(streams_of[1], (NODES,), ((0, 32),), -0.2, 0.2)), 0.01767767, 0.110485435)
    weight_in = noise(streams_of[2], (IN, HID), ((DEG / IN) ** 0.5), 6.0)
    weight_out = noise(streams_of[3], (HID, CLS), (8.0 / HID ** 0.5), 6.0)
    labels = set_ends(jax.random.randint(streams_of[4], (NODES,), 0, CLS), jax.random.fold_in(streams_of[4], 1), 0, CLS - 1).astype(jnp.int32)
    tile_slot = set_ends(jax.random.randint(streams_of[5], (DEVICES, TILES), 0, POSITIONS), jax.random.fold_in(streams_of[5], 1), 0, POSITIONS - 1).astype(jnp.int32)
    tile_edges = set_ends(jax.random.randint(streams_of[6], (DEVICES, TILES, 2, EPT), 0, TILE), jax.random.fold_in(streams_of[6], 1), 0, TILE - 1).astype(jnp.int32)
    tile_count = draw_tile_count(jax.random.fold_in(streams_of[8], 71), 0)
    return {"features": features, "norm_weight": norm_weight, "weight_in": weight_in, "weight_out": weight_out, "labels": labels, "tile_slot": tile_slot, "tile_edges": tile_edges, "tile_count": tile_count}


SOFTCAP = 15.0
LOSS_SCALE = 1024.0
HIGHEST = lax.Precision.HIGHEST


def dense_block(tile_slot, tile_edges, tile_count, device):
    slots_here = tile_slot[device]
    edges_here = tile_edges[device]
    row_group = NODE_DEV * N_COL
    col_group = NODE_DEV * N_ROW
    col_tiles = col_group // TILE
    target_rows = (slots_here // col_tiles)[:, None] * TILE + edges_here[:, 0, :]
    source_cols = (slots_here % col_tiles)[:, None] * TILE + edges_here[:, 1, :]
    flat_index = (target_rows * col_group + source_cols).reshape(-1).astype(jnp.int32)
    slot_live = (jnp.arange(TILES, dtype=jnp.int32) < tile_count[device]).astype(jnp.float32)
    edge_weights = jnp.broadcast_to(slot_live[:, None], target_rows.shape).reshape(-1)
    dense_tiles = jnp.zeros((row_group * col_group,), jnp.float32).at[flat_index].add(edge_weights)
    return dense_tiles.reshape(row_group, col_group)


def spread_forward(values, tile_slot, tile_edges, tile_count):
    feature_width = values.shape[1]
    node_grid = values.astype(jnp.float32).reshape(N_ROW, N_COL, NODE_DEV, feature_width)

    def per_row(row_index):
        def per_col(running, col_index):
            matrix = dense_block(tile_slot, tile_edges, tile_count, row_index * N_COL + col_index)
            source = node_grid[:, col_index].reshape(N_ROW * NODE_DEV, feature_width)
            return running + jnp.dot(matrix, source, preferred_element_type=jnp.float32, precision=HIGHEST), None

        running, _ = lax.scan(per_col, jnp.zeros((N_COL * NODE_DEV, feature_width), jnp.float32), jnp.arange(N_COL, dtype=jnp.int32))
        return running

    stacked = lax.map(per_row, jnp.arange(N_ROW, dtype=jnp.int32))
    return stacked.reshape(NODES, feature_width)


def spread_backward(values, tile_slot, tile_edges, tile_count):
    feature_width = values.shape[1]
    row_grid = values.astype(jnp.float32).reshape(N_ROW, N_COL * NODE_DEV, feature_width)

    def per_col(col_index):
        def per_row(running, row_index):
            matrix = dense_block(tile_slot, tile_edges, tile_count, row_index * N_COL + col_index)
            return running + jnp.dot(matrix.T, row_grid[row_index], preferred_element_type=jnp.float32, precision=HIGHEST), None

        running, _ = lax.scan(per_row, jnp.zeros((N_ROW * NODE_DEV, feature_width), jnp.float32), jnp.arange(N_ROW, dtype=jnp.int32))
        return running

    stacked = lax.map(per_col, jnp.arange(N_COL, dtype=jnp.int32))
    stacked = stacked.reshape(N_COL, N_ROW, NODE_DEV, feature_width).transpose(1, 0, 2, 3)
    return stacked.reshape(NODES, feature_width)


def reference(features, norm_weight, weight_in, weight_out, labels, tile_slot, tile_edges, tile_count):
    node_scale = norm_weight[:, None]
    normed = (node_scale * features.astype(jnp.float32)).astype(jnp.bfloat16)
    source_one = jnp.dot(normed, weight_in, preferred_element_type=jnp.float32)
    mixed_one = spread_forward(normed, tile_slot, tile_edges, tile_count)
    projected = jnp.dot(mixed_one, weight_in.astype(jnp.float32), precision=HIGHEST)
    pre_hidden = node_scale * (projected + source_one)
    hidden = jax.nn.relu(pre_hidden).astype(jnp.bfloat16)
    source_two = (node_scale * jnp.dot(hidden, weight_out, preferred_element_type=jnp.float32)).astype(jnp.bfloat16)
    logits = node_scale * (spread_forward(source_two, tile_slot, tile_edges, tile_count) + source_two.astype(jnp.float32))
    capped = SOFTCAP * jnp.tanh(logits / SOFTCAP)
    exp_capped = jnp.exp(capped)
    exp_total = jnp.sum(exp_capped, axis=1, keepdims=True)
    one_hot = (labels[:, None] == jnp.arange(CLS, dtype=jnp.int32)[None, :]).astype(jnp.float32)
    loss = jnp.sum(jnp.log(exp_total[:, 0]) - jnp.sum(capped * one_hot, axis=1)) / NODES
    d_logits = (LOSS_SCALE / NODES) * (exp_capped / exp_total - one_hot) * (1.0 - (capped / SOFTCAP) ** 2)
    back_two = (node_scale * d_logits).astype(jnp.bfloat16)
    d_source_two = node_scale * (spread_backward(back_two, tile_slot, tile_edges, tile_count) + back_two.astype(jnp.float32))
    grad_out = jnp.dot(hidden.astype(jnp.float32).T, d_source_two, precision=HIGHEST)
    d_hidden = jnp.dot(d_source_two, weight_out.astype(jnp.float32).T, precision=HIGHEST)
    back_one = (node_scale * jnp.where(pre_hidden > 0, d_hidden, 0.0)).astype(jnp.bfloat16)
    d_source_one = spread_backward(back_one, tile_slot, tile_edges, tile_count) + back_one.astype(jnp.float32)
    grad_in = jnp.dot(normed.astype(jnp.float32).T, d_source_one, precision=HIGHEST)
    return (grad_in, grad_out, loss)
```

```python
import functools

import jax
import jax.numpy as jnp
from jax import lax
from jax.experimental import pallas as pl
from jax.experimental.pallas import tpu as pltpu
from jax.sharding import PartitionSpec as P

TILE = 128
SOFTCAP = 15.0
LOSS_SCALE = 1024.0
UNROLL = 4
LOSS_ROWS = 16
MESH = pl.DeviceIdType.MESH
F32 = jnp.float32
BF16 = jnp.bfloat16
VMEM_LIMIT = 56 * 1024 * 1024


def dot(a, b, ca=1, cb=0):
    return lax.dot_general(a, b, (((ca,), (cb,)), ((), ())), preferred_element_type=F32)


def split2(x):
    hi = x.astype(BF16)
    return hi, (x - hi.astype(F32)).astype(BF16)


def densify_kernel(row_tiles, col_tiles, count_ref, slot_ref, edges_ref, out_ref, acc):
    places = row_tiles * col_tiles
    count = count_ref[0]
    acc[...] = jnp.zeros_like(acc)
    entries = edges_ref.shape[3]
    iota = lax.broadcasted_iota(jnp.int32, (TILE, entries), 0)

    def body(step, carry):
        found = []
        for u in range(UNROLL):
            s = step * UNROLL + u
            edges = edges_ref[0, s]
            rows = (iota == edges[0:1, :]).astype(F32).astype(BF16)
            cols = (iota == edges[1:2, :]).astype(F32).astype(BF16)
            found.append((jnp.where(s < count, slot_ref[0, s], places), dot(rows, cols, 1, 1)))
        for p, tile in found:
            acc[p] += tile
        return carry

    lax.fori_loop(0, (count + UNROLL - 1) // UNROLL, body, 0)
    for r in range(row_tiles):
        for c in range(col_tiles):
            out_ref[r * TILE : (r + 1) * TILE, c * TILE : (c + 1) * TILE] = acc[
                r * col_tiles + c
            ].astype(BF16)


def densify(tile_slot, tile_edges, tile_count, row_group, col_group):
    row_tiles, col_tiles = row_group // TILE, col_group // TILE
    return pl.pallas_call(
        functools.partial(densify_kernel, row_tiles, col_tiles),
        out_shape=jax.ShapeDtypeStruct((row_group, col_group), BF16),
        in_specs=[
            pl.BlockSpec(memory_space=pltpu.SMEM),
            pl.BlockSpec(memory_space=pltpu.SMEM),
            pl.BlockSpec(memory_space=pltpu.VMEM),
        ],
        out_specs=pl.BlockSpec(memory_space=pltpu.VMEM),
        scratch_shapes=[pltpu.VMEM((row_tiles * col_tiles + 1, TILE, TILE), F32)],
        compiler_params=pltpu.CompilerParams(vmem_limit_bytes=VMEM_LIMIT),
        name="densify",
    )(tile_count, tile_slot, tile_edges)


def step_kernel(
    R, C, nd, adj, feat, norm, w_in, w_out, labels,
    grad_in, grad_out, loss_out,
    gath_one, part_one, recv_one, gath_two, part_two, recv_two,
    gath_back, part_back, recv_back, part_grad, recv_grad, slots_grad, full_grad,
    send_sem, recv_sem,
):
    i = lax.axis_index("row")
    j = lax.axis_index("col")
    total_nodes = nd * R * C
    chunk = full_grad.shape[0] // C
    pending = []

    def row_peer(k):
        return (lax.rem(i + k, R), j)

    def col_peer(k):
        return (i, lax.rem(j + k, C))

    def send(phase, k, peer, src, dst):
        copy = pltpu.make_async_remote_copy(
            src_ref=src, dst_ref=dst,
            send_sem=send_sem.at[phase, k - 1], recv_sem=recv_sem.at[phase, k - 1],
            device_id=peer, device_id_type=MESH,
        )
        copy.start()
        pending.append(copy)
        return copy

    def arrive(copies):
        for copy in copies:
            copy.wait_recv()

    barrier = pltpu.get_barrier_semaphore()
    for k in range(1, R):
        pl.semaphore_signal(barrier, inc=1, device_id=row_peer(k), device_id_type=MESH)
    for k in range(1, C):
        pl.semaphore_signal(barrier, inc=1, device_id=col_peer(k), device_id_type=MESH)

    scale = jnp.transpose(jnp.broadcast_to(norm[...], (nd, nd)))
    normed = (scale * feat[...].astype(F32)).astype(BF16)
    mine = pl.ds(pl.multiple_of(i * nd, nd), nd)
    gath_one[mine, :] = normed
    pl.semaphore_wait(barrier, R + C - 2)

    def block_of(t):
        return adj[pl.ds(pl.multiple_of(t * nd, nd), nd), :]

    arrive([send(0, k, row_peer(k), gath_one.at[mine], gath_one.at[mine]) for k in range(1, R)])
    values = gath_one[...]
    copies = []
    for k in range(1, C):
        part_one[k - 1] = dot(block_of(lax.rem(j + k, C)), values)
        copies.append(send(1, k, col_peer(k), part_one.at[k - 1], recv_one.at[k - 1]))
    mixed = dot(block_of(j), values) + normed.astype(F32)
    for k in range(1, C):
        copies[k - 1].wait_recv()
        mixed = mixed + recv_one[k - 1]
    m_hi, m_lo = split2(mixed)
    m_least = (mixed - m_hi.astype(F32) - m_lo.astype(F32)).astype(BF16)
    w = w_in[...]
    pre_hidden = jnp.concatenate([scale, scale], axis=1) * (
        dot(m_hi, w) + (dot(m_lo, w) + dot(m_least, w))
    )
    hidden = jnp.maximum(pre_hidden, 0.0).astype(BF16)
    source_two = (scale * dot(hidden, w_out[...])).astype(BF16)
    gath_two[mine, :] = source_two
    arrive([send(2, k, row_peer(k), gath_two.at[mine], gath_two.at[mine]) for k in range(1, R)])
    values = gath_two[...]
    copies = []
    for k in range(1, C):
        part_two[k - 1] = dot(block_of(lax.rem(j + k, C)), values).astype(BF16)
        copies.append(send(3, k, col_peer(k), part_two.at[k - 1], recv_two.at[k - 1]))
    logits = dot(block_of(j), values) + source_two.astype(F32)
    for k in range(1, C):
        copies[k - 1].wait_recv()
        logits = logits + recv_two[k - 1].astype(F32)
    logits = scale * logits
    ratio = jnp.tanh(logits * (1.0 / SOFTCAP))
    capped = SOFTCAP * ratio
    exp_capped = jnp.exp(capped)
    exp_total = jnp.sum(exp_capped, axis=1, keepdims=True)
    label_rows = jnp.transpose(jnp.broadcast_to(labels[...].astype(F32), (nd, nd)))
    one_hot = jnp.where(
        label_rows == lax.broadcasted_iota(jnp.int32, (nd, nd), 1).astype(F32), 1.0, 0.0
    )
    node_loss = jnp.log(exp_total) - jnp.sum(capped * one_hot, axis=1, keepdims=True)
    loss_local = jnp.sum(node_loss, axis=0, keepdims=True)
    d_logits = (LOSS_SCALE / total_nodes) * (exp_capped / exp_total - one_hot) * (
        1.0 - ratio * ratio
    )
    back_two = (scale * d_logits).astype(BF16)

    upper = lax.broadcasted_iota(jnp.int32, (LOSS_ROWS, TILE), 0) < LOSS_ROWS // 2

    def loss_rows(value):
        value = jnp.broadcast_to(value, (LOSS_ROWS, TILE))
        hi, lo = split2(value)
        return jnp.where(upper, hi.astype(F32), lo.astype(F32)).astype(BF16)

    def read_loss(rows):
        rows = rows.astype(F32)
        return rows[0:1, :] + rows[LOSS_ROWS // 2 : LOSS_ROWS // 2 + 1, :]

    gath_back[j, :nd, :] = back_two
    gath_back[j, nd:, :] = loss_rows(loss_local)
    arrive([send(4, k, col_peer(k), gath_back.at[j], gath_back.at[j]) for k in range(1, C)])
    loss_col = read_loss(gath_back[0, nd:, :])
    for k in range(1, C):
        loss_col = loss_col + read_loss(gath_back[k, nd:, :])
    values_t = jnp.transpose(
        jnp.concatenate([gath_back[k, :nd, :] for k in range(C)], axis=0).astype(F32)
    ).astype(BF16)
    rows_loss = loss_rows(loss_col)

    def back_of(t):
        return dot(values_t, adj[:, pl.ds(pl.multiple_of(t * nd, nd), nd)])

    copies = []
    for k in range(1, R):
        part_back[k - 1, :nd, :] = back_of(lax.rem(i + k, R)).astype(BF16)
        part_back[k - 1, nd:, :] = rows_loss
        copies.append(send(5, k, row_peer(k), part_back.at[k - 1], recv_back.at[i]))
    recv_back[i, nd:, :] = rows_loss
    summed = back_of(i)
    arrive(copies)
    recv_back[i, :nd, :] = jnp.zeros((nd, nd), BF16)
    loss_all = read_loss(recv_back[0, nd:, :])
    for k in range(1, R):
        loss_all = loss_all + read_loss(recv_back[k, nd:, :])
    for k in range(R):
        summed = summed + recv_back[k, :nd, :].astype(F32)
    loss_out[...] = jnp.broadcast_to(loss_all * (1.0 / total_nodes), loss_out.shape)
    d_source = scale * (jnp.transpose(summed) + back_two.astype(F32))
    d_hi, d_lo = split2(d_source)
    d_hidden = dot(d_hi, w_out[...], 1, 1) + dot(d_lo, w_out[...], 1, 1)
    back_one = jnp.where(
        pre_hidden > 0, jnp.concatenate([scale, scale], axis=1) * d_hidden, 0.0
    ).astype(BF16)
    local_out = dot(hidden, d_hi, 0, 0) + dot(hidden, d_lo, 0, 0)
    local_in = dot(m_hi, back_one, 0, 0) + dot(m_lo, back_one, 0, 0)

    fan_in, half = local_in.shape[0], TILE
    hid = local_in.shape[1]
    for h in range(hid // half):
        part_grad[h * fan_in : (h + 1) * fan_in, :] = local_in[:, h * half : (h + 1) * half].astype(
            BF16
        )
    base = fan_in * (hid // half)
    part_grad[base:, :] = local_out.astype(BF16)

    def rows_of(t):
        return pl.ds(pl.multiple_of(t * chunk, chunk), chunk)

    copies = [
        send(6, k, col_peer(k), part_grad.at[rows_of(lax.rem(j + k, C))], recv_grad.at[k - 1])
        for k in range(1, C)
    ]
    total = part_grad[rows_of(j), :].astype(F32)
    for k in range(1, C):
        copies[k - 1].wait_recv()
        total = total + recv_grad[k - 1].astype(F32)
    slots_grad[i] = total.astype(BF16)
    arrive([send(7, k, row_peer(k), slots_grad.at[i], slots_grad.at[i]) for k in range(1, R)])
    total = slots_grad[0].astype(F32)
    for k in range(1, R):
        total = total + slots_grad[k].astype(F32)
    full_grad[rows_of(j), :] = total.astype(BF16)
    arrive(
        [
            send(8, k, col_peer(k), full_grad.at[rows_of(j)], full_grad.at[rows_of(j)])
            for k in range(1, C)
        ]
    )
    for h in range(hid // half):
        grad_in[:, h * half : (h + 1) * half] = full_grad[h * fan_in : (h + 1) * fan_in, :].astype(
            F32
        )
    grad_out[...] = full_grad[base:, :].astype(F32)
    for copy in pending:
        copy.wait_send()


def per_device(
    features, norm_weight, weight_in, weight_out, labels, tile_slot, tile_edges, tile_count
):
    R = lax.axis_size("row")
    C = lax.axis_size("col")
    nd, fan_in = features.shape
    hid, classes = weight_out.shape
    adjacency = densify(tile_slot, tile_edges, tile_count, nd * C, nd * R)
    grad_rows = (fan_in * hid + hid * classes) // TILE
    chunk = grad_rows // C
    most = max(R, C) - 1
    vmem = pl.BlockSpec(memory_space=pltpu.VMEM)
    grad_in, grad_out, loss = pl.pallas_call(
        functools.partial(step_kernel, R, C, nd),
        out_shape=(
            jax.ShapeDtypeStruct((fan_in, hid), F32),
            jax.ShapeDtypeStruct((hid, classes), F32),
            jax.ShapeDtypeStruct((1, TILE), F32),
        ),
        in_specs=[vmem] * 6,
        out_specs=(vmem, vmem, vmem),
        scratch_shapes=[
            pltpu.VMEM((R * nd, fan_in), BF16),
            pltpu.VMEM((C - 1, nd, fan_in), F32),
            pltpu.VMEM((C - 1, nd, fan_in), F32),
            pltpu.VMEM((R * nd, classes), BF16),
            pltpu.VMEM((C - 1, nd, classes), BF16),
            pltpu.VMEM((C - 1, nd, classes), BF16),
            pltpu.VMEM((C, nd + LOSS_ROWS, classes), BF16),
            pltpu.VMEM((R - 1, nd + LOSS_ROWS, classes), BF16),
            pltpu.VMEM((R, nd + LOSS_ROWS, classes), BF16),
            pltpu.VMEM((grad_rows, TILE), BF16),
            pltpu.VMEM((C - 1, chunk, TILE), BF16),
            pltpu.VMEM((R, chunk, TILE), BF16),
            pltpu.VMEM((grad_rows, TILE), BF16),
            pltpu.SemaphoreType.DMA((9, most)),
            pltpu.SemaphoreType.DMA((9, most)),
        ],
        compiler_params=pltpu.CompilerParams(
            collective_id=0, has_side_effects=True, vmem_limit_bytes=VMEM_LIMIT
        ),
        name="train_step",
    )(adjacency, features, norm_weight[None, :], weight_in, weight_out, labels[None, :])
    return grad_in, grad_out, loss[0, 0]


def solution(mesh):
    in_specs = (
        P(("row", "col"), None),
        P(("row", "col")),
        P(),
        P(),
        P(("row", "col")),
        P(("row", "col"), None),
        P(("row", "col"), None, None, None),
        P(("row", "col")),
    )
    out_specs = (P(), P(), P())
    return jax.shard_map(
        per_device, mesh=mesh, in_specs=in_specs, out_specs=out_specs, check_vma=False
    )
```

```python
import functools

import jax
import jax.numpy as jnp
from jax import lax
from jax.experimental import pallas as pl
from jax.experimental.pallas import tpu as pltpu
from jax.sharding import PartitionSpec as P

TILE = 128
SOFTCAP = 15.0
LOSS_SCALE = 1024.0
UNROLL = 16
LOSS_ROWS = 16
MESH = pl.DeviceIdType.MESH
F32 = jnp.float32
BF16 = jnp.bfloat16
VMEM_LIMIT = 56 * 1024 * 1024


def dot(a, b, ca=1, cb=0):
    return lax.dot_general(a, b, (((ca,), (cb,)), ((), ())), preferred_element_type=F32)


def split2(x):
    hi = x.astype(BF16)
    return hi, (x - hi.astype(F32)).astype(BF16)


def densify_kernel(row_tiles, col_tiles, count_ref, slot_ref, edges_ref, out_ref, acc):
    places = row_tiles * col_tiles
    count = count_ref[0]
    acc[...] = jnp.zeros_like(acc)
    entries = edges_ref.shape[3]
    iota = lax.broadcasted_iota(jnp.int32, (TILE, entries), 0)

    def body(step, carry):
        found = []
        for u in range(UNROLL):
            s = step * UNROLL + u
            edges = edges_ref[0, s]
            rows = (iota == edges[0:1, :]).astype(F32).astype(BF16)
            cols = (iota == edges[1:2, :]).astype(F32).astype(BF16)
            found.append((jnp.where(s < count, slot_ref[0, s], places), dot(rows, cols, 1, 1)))
        for p, tile in found:
            acc[p] += tile
        return carry

    lax.fori_loop(0, (count + UNROLL - 1) // UNROLL, body, 0)
    for r in range(row_tiles):
        for c in range(col_tiles):
            out_ref[r * TILE : (r + 1) * TILE, c * TILE : (c + 1) * TILE] = acc[
                r * col_tiles + c
            ].astype(BF16)


def densify(tile_slot, tile_edges, tile_count, row_group, col_group):
    row_tiles, col_tiles = row_group // TILE, col_group // TILE
    return pl.pallas_call(
        functools.partial(densify_kernel, row_tiles, col_tiles),
        out_shape=jax.ShapeDtypeStruct((row_group, col_group), BF16),
        in_specs=[
            pl.BlockSpec(memory_space=pltpu.SMEM),
            pl.BlockSpec(memory_space=pltpu.SMEM),
            pl.BlockSpec(memory_space=pltpu.VMEM),
        ],
        out_specs=pl.BlockSpec(memory_space=pltpu.VMEM),
        scratch_shapes=[pltpu.VMEM((row_tiles * col_tiles + 1, TILE, TILE), F32)],
        compiler_params=pltpu.CompilerParams(vmem_limit_bytes=VMEM_LIMIT),
        name="densify",
    )(tile_count, tile_slot, tile_edges)


def step_kernel(
    R, C, nd, adj, feat, norm, w_in, w_out, labels,
    grad_in, grad_out, loss_out,
    gath_one, part_one, recv_one, part_low, recv_low, gath_two, part_two, recv_two,
    gath_back, part_back, recv_back, part_grad, recv_grad, slots_grad, full_grad,
    send_sem, recv_sem,
):
    i = lax.axis_index("row")
    j = lax.axis_index("col")
    total_nodes = nd * R * C
    chunk = full_grad.shape[0] // C
    pending = []

    def row_peer(k):
        return (lax.rem(i + k, R), j)

    def col_peer(k):
        return (i, lax.rem(j + k, C))

    def send(phase, k, peer, src, dst):
        copy = pltpu.make_async_remote_copy(
            src_ref=src, dst_ref=dst,
            send_sem=send_sem.at[phase, k - 1], recv_sem=recv_sem.at[phase, k - 1],
            device_id=peer, device_id_type=MESH,
        )
        copy.start()
        pending.append(copy)
        return copy

    def arrive(copies):
        for copy in copies:
            copy.wait_recv()

    barrier = pltpu.get_barrier_semaphore()
    for k in range(1, R):
        pl.semaphore_signal(barrier, inc=1, device_id=row_peer(k), device_id_type=MESH)
    for k in range(1, C):
        pl.semaphore_signal(barrier, inc=1, device_id=col_peer(k), device_id_type=MESH)

    scale = jnp.transpose(jnp.broadcast_to(norm[...], (nd, nd)))
    normed = (scale * feat[...].astype(F32)).astype(BF16)
    mine = pl.ds(pl.multiple_of(i * nd, nd), nd)
    gath_one[mine, :] = normed
    pl.semaphore_wait(barrier, R + C - 2)

    def block_of(t):
        return adj[pl.ds(pl.multiple_of(t * nd, nd), nd), :]

    arrive([send(0, k, row_peer(k), gath_one.at[mine], gath_one.at[mine]) for k in range(1, R)])
    values = gath_one[...]
    copies = []
    for k in range(1, C):
        part_one[k - 1], part_low[k - 1] = split2(dot(block_of(lax.rem(j + k, C)), values))
        copies.append(send(1, k, col_peer(k), part_one.at[k - 1], recv_one.at[k - 1]))
    low_copies = [
        send(9, k, col_peer(k), part_low.at[k - 1], recv_low.at[k - 1]) for k in range(1, C)
    ]
    mixed = dot(block_of(j), values) + normed.astype(F32)
    for k in range(1, C):
        copies[k - 1].wait_recv()
        mixed = mixed + recv_one[k - 1].astype(F32)
    w = w_in[...]
    scale_wide = jnp.concatenate([scale, scale], axis=1)
    m_hi, m_lo = split2(mixed)
    hidden_ahead = jnp.maximum(scale_wide * (dot(m_hi, w) + dot(m_lo, w)), 0.0).astype(BF16)
    source_two = (scale * dot(hidden_ahead, w_out[...])).astype(BF16)
    gath_two[mine, :] = source_two
    arrive([send(2, k, row_peer(k), gath_two.at[mine], gath_two.at[mine]) for k in range(1, R)])
    values = gath_two[...]
    copies = []
    for k in range(1, C):
        part_two[k - 1] = dot(block_of(lax.rem(j + k, C)), values).astype(BF16)
        copies.append(send(3, k, col_peer(k), part_two.at[k - 1], recv_two.at[k - 1]))
    logits = dot(block_of(j), values) + source_two.astype(F32)
    for k in range(1, C):
        copies[k - 1].wait_recv()
        logits = logits + recv_two[k - 1].astype(F32)
    logits = scale * logits
    ratio = jnp.tanh(logits * (1.0 / SOFTCAP))
    capped = SOFTCAP * ratio
    exp_capped = jnp.exp(capped)
    exp_total = jnp.sum(exp_capped, axis=1, keepdims=True)
    label_rows = jnp.transpose(jnp.broadcast_to(labels[...].astype(F32), (nd, nd)))
    one_hot = jnp.where(
        label_rows == lax.broadcasted_iota(jnp.int32, (nd, nd), 1).astype(F32), 1.0, 0.0
    )
    node_loss = jnp.log(exp_total) - jnp.sum(capped * one_hot, axis=1, keepdims=True)
    loss_local = jnp.sum(node_loss, axis=0, keepdims=True)
    d_logits = (LOSS_SCALE / total_nodes) * (exp_capped / exp_total - one_hot) * (
        1.0 - ratio * ratio
    )
    back_two = (scale * d_logits).astype(BF16)

    upper = lax.broadcasted_iota(jnp.int32, (LOSS_ROWS, TILE), 0) < LOSS_ROWS // 2

    def loss_rows(value):
        value = jnp.broadcast_to(value, (LOSS_ROWS, TILE))
        hi, lo = split2(value)
        return jnp.where(upper, hi.astype(F32), lo.astype(F32)).astype(BF16)

    def read_loss(rows):
        rows = rows.astype(F32)
        return rows[0:1, :] + rows[LOSS_ROWS // 2 : LOSS_ROWS // 2 + 1, :]

    gath_back[j, :nd, :] = back_two
    gath_back[j, nd:, :] = loss_rows(loss_local)
    copies = [send(4, k, col_peer(k), gath_back.at[j], gath_back.at[j]) for k in range(1, C)]
    arrive(low_copies)
    low = recv_low[0].astype(F32)
    for k in range(2, C):
        low = low + recv_low[k - 1].astype(F32)
    mixed = mixed + low
    m_hi, m_lo = split2(mixed)
    m_least = (mixed - m_hi.astype(F32) - m_lo.astype(F32)).astype(BF16)
    pre_hidden = scale_wide * (dot(m_hi, w) + (dot(m_lo, w) + dot(m_least, w)))
    hidden = jnp.maximum(pre_hidden, 0.0).astype(BF16)
    arrive(copies)
    loss_col = read_loss(gath_back[0, nd:, :])
    for k in range(1, C):
        loss_col = loss_col + read_loss(gath_back[k, nd:, :])
    values_t = jnp.transpose(
        jnp.concatenate([gath_back[k, :nd, :] for k in range(C)], axis=0).astype(F32)
    ).astype(BF16)
    rows_loss = loss_rows(loss_col)

    def back_of(t):
        return dot(values_t, adj[:, pl.ds(pl.multiple_of(t * nd, nd), nd)])

    copies = []
    for k in range(1, R):
        part_back[k - 1, :nd, :] = back_of(lax.rem(i + k, R)).astype(BF16)
        part_back[k - 1, nd:, :] = rows_loss
        copies.append(send(5, k, row_peer(k), part_back.at[k - 1], recv_back.at[i]))
    recv_back[i, nd:, :] = rows_loss
    summed = back_of(i)
    arrive(copies)
    recv_back[i, :nd, :] = jnp.zeros((nd, nd), BF16)
    loss_all = read_loss(recv_back[0, nd:, :])
    for k in range(1, R):
        loss_all = loss_all + read_loss(recv_back[k, nd:, :])
    for k in range(R):
        summed = summed + recv_back[k, :nd, :].astype(F32)
    loss_out[...] = jnp.broadcast_to(loss_all * (1.0 / total_nodes), loss_out.shape)
    d_source = scale * (jnp.transpose(summed) + back_two.astype(F32))
    d_hi, d_lo = split2(d_source)
    d_hidden = dot(d_hi, w_out[...], 1, 1) + dot(d_lo, w_out[...], 1, 1)
    back_one = jnp.where(
        pre_hidden > 0, scale_wide * d_hidden, 0.0
    ).astype(BF16)
    local_out = dot(hidden, d_hi, 0, 0) + dot(hidden, d_lo, 0, 0)
    local_in = dot(m_hi, back_one, 0, 0) + dot(m_lo, back_one, 0, 0)

    fan_in, half = local_in.shape[0], TILE
    hid = local_in.shape[1]
    for h in range(hid // half):
        part_grad[h * fan_in : (h + 1) * fan_in, :] = local_in[:, h * half : (h + 1) * half].astype(
            BF16
        )
    base = fan_in * (hid // half)
    part_grad[base:, :] = local_out.astype(BF16)

    def rows_of(t):
        return pl.ds(pl.multiple_of(t * chunk, chunk), chunk)

    copies = [
        send(6, k, col_peer(k), part_grad.at[rows_of(lax.rem(j + k, C))], recv_grad.at[k - 1])
        for k in range(1, C)
    ]
    total = part_grad[rows_of(j), :].astype(F32)
    for k in range(1, C):
        copies[k - 1].wait_recv()
        total = total + recv_grad[k - 1].astype(F32)
    slots_grad[i] = total.astype(BF16)
    arrive([send(7, k, row_peer(k), slots_grad.at[i], slots_grad.at[i]) for k in range(1, R)])
    total = slots_grad[0].astype(F32)
    for k in range(1, R):
        total = total + slots_grad[k].astype(F32)
    full_grad[rows_of(j), :] = total.astype(BF16)
    arrive(
        [
            send(8, k, col_peer(k), full_grad.at[rows_of(j)], full_grad.at[rows_of(j)])
            for k in range(1, C)
        ]
    )
    for h in range(hid // half):
        grad_in[:, h * half : (h + 1) * half] = full_grad[h * fan_in : (h + 1) * fan_in, :].astype(
            F32
        )
    grad_out[...] = full_grad[base:, :].astype(F32)
    for copy in pending:
        copy.wait_send()


def per_device(
    features, norm_weight, weight_in, weight_out, labels, tile_slot, tile_edges, tile_count
):
    R = lax.axis_size("row")
    C = lax.axis_size("col")
    nd, fan_in = features.shape
    hid, classes = weight_out.shape
    adjacency = densify(tile_slot, tile_edges, tile_count, nd * C, nd * R)
    grad_rows = (fan_in * hid + hid * classes) // TILE
    chunk = grad_rows // C
    most = max(R, C) - 1
    vmem = pl.BlockSpec(memory_space=pltpu.VMEM)
    grad_in, grad_out, loss = pl.pallas_call(
        functools.partial(step_kernel, R, C, nd),
        out_shape=(
            jax.ShapeDtypeStruct((fan_in, hid), F32),
            jax.ShapeDtypeStruct((hid, classes), F32),
            jax.ShapeDtypeStruct((1, TILE), F32),
        ),
        in_specs=[vmem] * 6,
        out_specs=(vmem, vmem, vmem),
        scratch_shapes=[
            pltpu.VMEM((R * nd, fan_in), BF16),
            pltpu.VMEM((C - 1, nd, fan_in), BF16),
            pltpu.VMEM((C - 1, nd, fan_in), BF16),
            pltpu.VMEM((C - 1, nd, fan_in), BF16),
            pltpu.VMEM((C - 1, nd, fan_in), BF16),
            pltpu.VMEM((R * nd, classes), BF16),
            pltpu.VMEM((C - 1, nd, classes), BF16),
            pltpu.VMEM((C - 1, nd, classes), BF16),
            pltpu.VMEM((C, nd + LOSS_ROWS, classes), BF16),
            pltpu.VMEM((R - 1, nd + LOSS_ROWS, classes), BF16),
            pltpu.VMEM((R, nd + LOSS_ROWS, classes), BF16),
            pltpu.VMEM((grad_rows, TILE), BF16),
            pltpu.VMEM((C - 1, chunk, TILE), BF16),
            pltpu.VMEM((R, chunk, TILE), BF16),
            pltpu.VMEM((grad_rows, TILE), BF16),
            pltpu.SemaphoreType.DMA((10, most)),
            pltpu.SemaphoreType.DMA((10, most)),
        ],
        compiler_params=pltpu.CompilerParams(
            collective_id=0, has_side_effects=True, vmem_limit_bytes=VMEM_LIMIT
        ),
        name="train_step",
    )(adjacency, features, norm_weight[None, :], weight_in, weight_out, labels[None, :])
    return grad_in, grad_out, loss[0, 0]


def solution(mesh):
    in_specs = (
        P(("row", "col"), None),
        P(("row", "col")),
        P(),
        P(),
        P(("row", "col")),
        P(("row", "col"), None),
        P(("row", "col"), None, None, None),
        P(("row", "col")),
    )
    out_specs = (P(), P(), P())
    return jax.shard_map(
        per_device, mesh=mesh, in_specs=in_specs, out_specs=out_specs, check_vma=False
    )
```

```python
import functools

import jax
import jax.numpy as jnp
from jax import lax
from jax.experimental import pallas as pl
from jax.experimental.pallas import tpu as pltpu
from jax.sharding import PartitionSpec as P

TILE = 128
SOFTCAP = 15.0
LOSS_SCALE = 1024.0
UNROLL = 32
LOSS_ROWS = 16
MESH = pl.DeviceIdType.MESH
F32 = jnp.float32
BF16 = jnp.bfloat16
VMEM_LIMIT = 56 * 1024 * 1024


def dot(a, b, ca=1, cb=0):
    return lax.dot_general(a, b, (((ca,), (cb,)), ((), ())), preferred_element_type=F32)


def split2(x):
    hi = x.astype(BF16)
    return hi, (x - hi.astype(F32)).astype(BF16)


def densify_kernel(row_tiles, col_tiles, count_ref, slot_ref, edges_ref, out_ref, acc):
    places = row_tiles * col_tiles
    count = count_ref[0]
    acc[...] = jnp.zeros_like(acc)
    entries = edges_ref.shape[3]
    iota = lax.broadcasted_iota(jnp.int32, (TILE, entries), 0).astype(F32).astype(BF16)
    ones, zeros = jnp.ones(iota.shape, BF16), jnp.zeros(iota.shape, BF16)

    def body(step, carry):
        found = []
        for u in range(UNROLL):
            s = step * UNROLL + u
            edges = edges_ref[0, s].astype(F32).astype(BF16)
            rows = jnp.where(iota == edges[0:1, :], ones, zeros)
            cols = jnp.where(iota == edges[1:2, :], ones, zeros)
            found.append((jnp.where(s < count, slot_ref[0, s], places), dot(rows, cols, 1, 1)))
        for p, tile in found:
            acc[p] += tile
        return carry

    lax.fori_loop(0, (count + UNROLL - 1) // UNROLL, body, 0)
    for r in range(row_tiles):
        for c in range(col_tiles):
            out_ref[r * TILE : (r + 1) * TILE, c * TILE : (c + 1) * TILE] = acc[
                r * col_tiles + c
            ].astype(BF16)


def densify(tile_slot, tile_edges, tile_count, row_group, col_group):
    row_tiles, col_tiles = row_group // TILE, col_group // TILE
    return pl.pallas_call(
        functools.partial(densify_kernel, row_tiles, col_tiles),
        out_shape=jax.ShapeDtypeStruct((row_group, col_group), BF16),
        in_specs=[
            pl.BlockSpec(memory_space=pltpu.SMEM),
            pl.BlockSpec(memory_space=pltpu.SMEM),
            pl.BlockSpec(memory_space=pltpu.VMEM),
        ],
        out_specs=pl.BlockSpec(memory_space=pltpu.VMEM),
        scratch_shapes=[pltpu.VMEM((row_tiles * col_tiles + 1, TILE, TILE), F32)],
        compiler_params=pltpu.CompilerParams(vmem_limit_bytes=VMEM_LIMIT),
        name="densify",
    )(tile_count, tile_slot, tile_edges)


def step_kernel(
    R, C, nd, adj, feat, norm, w_in, w_out, labels,
    grad_in, grad_out, loss_out,
    gath_one, part_one, recv_one, part_low, recv_low, gath_two, part_two, recv_two,
    gath_back, part_back, recv_back, part_grad, recv_grad, slots_grad, full_grad,
    send_sem, recv_sem,
):
    i = lax.axis_index("row")
    j = lax.axis_index("col")
    total_nodes = nd * R * C
    chunk = full_grad.shape[0] // C
    pending = []

    def row_peer(k):
        return (lax.rem(i + k, R), j)

    def col_peer(k):
        return (i, lax.rem(j + k, C))

    def send(phase, k, peer, src, dst):
        copy = pltpu.make_async_remote_copy(
            src_ref=src, dst_ref=dst,
            send_sem=send_sem.at[phase, k - 1], recv_sem=recv_sem.at[phase, k - 1],
            device_id=peer, device_id_type=MESH,
        )
        copy.start()
        pending.append(copy)
        return copy

    def arrive(copies):
        for copy in copies:
            copy.wait_recv()

    barrier = pltpu.get_barrier_semaphore()
    for k in range(1, R):
        pl.semaphore_signal(barrier, inc=1, device_id=row_peer(k), device_id_type=MESH)
    for k in range(1, C):
        pl.semaphore_signal(barrier, inc=1, device_id=col_peer(k), device_id_type=MESH)

    scale = jnp.transpose(jnp.broadcast_to(norm[...], (nd, nd)))
    normed = (scale * feat[...].astype(F32)).astype(BF16)
    mine = pl.ds(pl.multiple_of(i * nd, nd), nd)
    gath_one[mine, :] = normed
    pl.semaphore_wait(barrier, R + C - 2)

    def block_of(t):
        return adj[pl.ds(pl.multiple_of(t * nd, nd), nd), :]

    arrive([send(0, k, row_peer(k), gath_one.at[mine], gath_one.at[mine]) for k in range(1, R)])
    values = gath_one[...]
    copies = []
    for k in range(1, C):
        part_one[k - 1], part_low[k - 1] = split2(dot(block_of(lax.rem(j + k, C)), values))
        copies.append(send(1, k, col_peer(k), part_one.at[k - 1], recv_one.at[k - 1]))
    low_copies = [
        send(9, k, col_peer(k), part_low.at[k - 1], recv_low.at[k - 1]) for k in range(1, C)
    ]
    mixed = dot(block_of(j), values) + normed.astype(F32)
    for k in range(1, C):
        copies[k - 1].wait_recv()
        mixed = mixed + recv_one[k - 1].astype(F32)
    w = w_in[...]
    scale_wide = jnp.concatenate([scale, scale], axis=1)
    m_hi, m_lo = split2(mixed)
    hidden_ahead = jnp.maximum(scale_wide * (dot(m_hi, w) + dot(m_lo, w)), 0.0).astype(BF16)
    source_two = (scale * dot(hidden_ahead, w_out[...])).astype(BF16)
    gath_two[mine, :] = source_two
    arrive([send(2, k, row_peer(k), gath_two.at[mine], gath_two.at[mine]) for k in range(1, R)])
    values = gath_two[...]
    copies = []
    for k in range(1, C):
        part_two[k - 1] = dot(block_of(lax.rem(j + k, C)), values).astype(BF16)
        copies.append(send(3, k, col_peer(k), part_two.at[k - 1], recv_two.at[k - 1]))
    logits = dot(block_of(j), values) + source_two.astype(F32)
    for k in range(1, C):
        copies[k - 1].wait_recv()
        logits = logits + recv_two[k - 1].astype(F32)
    logits = scale * logits
    ratio = jnp.tanh(logits * (1.0 / SOFTCAP))
    capped = SOFTCAP * ratio
    exp_capped = jnp.exp(capped)
    exp_total = jnp.sum(exp_capped, axis=1, keepdims=True)
    label_rows = jnp.transpose(jnp.broadcast_to(labels[...].astype(F32), (nd, nd)))
    one_hot = jnp.where(
        label_rows == lax.broadcasted_iota(jnp.int32, (nd, nd), 1).astype(F32), 1.0, 0.0
    )
    node_loss = jnp.log(exp_total) - jnp.sum(capped * one_hot, axis=1, keepdims=True)
    loss_local = jnp.sum(node_loss, axis=0, keepdims=True)
    d_logits = (LOSS_SCALE / total_nodes) * (exp_capped / exp_total - one_hot) * (
        1.0 - ratio * ratio
    )
    back_two = (scale * d_logits).astype(BF16)

    upper = lax.broadcasted_iota(jnp.int32, (LOSS_ROWS, TILE), 0) < LOSS_ROWS // 2

    def loss_rows(value):
        value = jnp.broadcast_to(value, (LOSS_ROWS, TILE))
        hi, lo = split2(value)
        return jnp.where(upper, hi.astype(F32), lo.astype(F32)).astype(BF16)

    def read_loss(rows):
        rows = rows.astype(F32)
        return rows[0:1, :] + rows[LOSS_ROWS // 2 : LOSS_ROWS // 2 + 1, :]

    gath_back[j, :nd, :] = back_two
    gath_back[j, nd:, :] = loss_rows(loss_local)
    copies = [send(4, k, col_peer(k), gath_back.at[j], gath_back.at[j]) for k in range(1, C)]
    arrive(low_copies)
    low = recv_low[0].astype(F32)
    for k in range(2, C):
        low = low + recv_low[k - 1].astype(F32)
    mixed = mixed + low
    m_hi, m_lo = split2(mixed)
    m_least = (mixed - m_hi.astype(F32) - m_lo.astype(F32)).astype(BF16)
    pre_hidden = scale_wide * (dot(m_hi, w) + (dot(m_lo, w) + dot(m_least, w)))
    hidden = jnp.maximum(pre_hidden, 0.0).astype(BF16)
    arrive(copies)
    loss_col = read_loss(gath_back[0, nd:, :])
    for k in range(1, C):
        loss_col = loss_col + read_loss(gath_back[k, nd:, :])
    values_t = jnp.transpose(
        jnp.concatenate([gath_back[k, :nd, :] for k in range(C)], axis=0).astype(F32)
    ).astype(BF16)
    rows_loss = loss_rows(loss_col)

    def back_of(t):
        return dot(values_t, adj[:, pl.ds(pl.multiple_of(t * nd, nd), nd)])

    copies = []
    for k in range(1, R):
        part_back[k - 1, :nd, :] = back_of(lax.rem(i + k, R)).astype(BF16)
        part_back[k - 1, nd:, :] = rows_loss
        copies.append(send(5, k, row_peer(k), part_back.at[k - 1], recv_back.at[i]))
    recv_back[i, nd:, :] = rows_loss
    summed = back_of(i)
    arrive(copies)
    recv_back[i, :nd, :] = jnp.zeros((nd, nd), BF16)
    loss_all = read_loss(recv_back[0, nd:, :])
    for k in range(1, R):
        loss_all = loss_all + read_loss(recv_back[k, nd:, :])
    for k in range(R):
        summed = summed + recv_back[k, :nd, :].astype(F32)
    loss_out[...] = jnp.broadcast_to(loss_all * (1.0 / total_nodes), loss_out.shape)
    d_source = scale * (jnp.transpose(summed) + back_two.astype(F32))
    d_hi, d_lo = split2(d_source)
    d_hidden = dot(d_hi, w_out[...], 1, 1) + dot(d_lo, w_out[...], 1, 1)
    back_one = jnp.where(
        pre_hidden > 0, scale_wide * d_hidden, 0.0
    ).astype(BF16)
    local_out = dot(hidden, d_hi, 0, 0) + dot(hidden, d_lo, 0, 0)
    local_in = dot(m_hi, back_one, 0, 0) + dot(m_lo, back_one, 0, 0)

    fan_in, half = local_in.shape[0], TILE
    hid = local_in.shape[1]
    for h in range(hid // half):
        part_grad[h * fan_in : (h + 1) * fan_in, :] = local_in[:, h * half : (h + 1) * half].astype(
            BF16
        )
    base = fan_in * (hid // half)
    part_grad[base:, :] = local_out.astype(BF16)

    def rows_of(t):
        return pl.ds(pl.multiple_of(t * chunk, chunk), chunk)

    copies = [
        send(6, k, col_peer(k), part_grad.at[rows_of(lax.rem(j + k, C))], recv_grad.at[k - 1])
        for k in range(1, C)
    ]
    total = part_grad[rows_of(j), :].astype(F32)
    for k in range(1, C):
        copies[k - 1].wait_recv()
        total = total + recv_grad[k - 1].astype(F32)
    slots_grad[i] = total.astype(BF16)
    arrive([send(7, k, row_peer(k), slots_grad.at[i], slots_grad.at[i]) for k in range(1, R)])
    total = slots_grad[0].astype(F32)
    for k in range(1, R):
        total = total + slots_grad[k].astype(F32)
    full_grad[rows_of(j), :] = total.astype(BF16)
    arrive(
        [
            send(8, k, col_peer(k), full_grad.at[rows_of(j)], full_grad.at[rows_of(j)])
            for k in range(1, C)
        ]
    )
    for h in range(hid // half):
        grad_in[:, h * half : (h + 1) * half] = full_grad[h * fan_in : (h + 1) * fan_in, :].astype(
            F32
        )
    grad_out[...] = full_grad[base:, :].astype(F32)
    for copy in pending:
        copy.wait_send()


def per_device(
    features, norm_weight, weight_in, weight_out, labels, tile_slot, tile_edges, tile_count
):
    R = lax.axis_size("row")
    C = lax.axis_size("col")
    nd, fan_in = features.shape
    hid, classes = weight_out.shape
    adjacency = densify(tile_slot, tile_edges, tile_count, nd * C, nd * R)
    grad_rows = (fan_in * hid + hid * classes) // TILE
    chunk = grad_rows // C
    most = max(R, C) - 1
    vmem = pl.BlockSpec(memory_space=pltpu.VMEM)
    grad_in, grad_out, loss = pl.pallas_call(
        functools.partial(step_kernel, R, C, nd),
        out_shape=(
            jax.ShapeDtypeStruct((fan_in, hid), F32),
            jax.ShapeDtypeStruct((hid, classes), F32),
            jax.ShapeDtypeStruct((1, TILE), F32),
        ),
        in_specs=[vmem] * 6,
        out_specs=(vmem, vmem, vmem),
        scratch_shapes=[
            pltpu.VMEM((R * nd, fan_in), BF16),
            pltpu.VMEM((C - 1, nd, fan_in), BF16),
            pltpu.VMEM((C - 1, nd, fan_in), BF16),
            pltpu.VMEM((C - 1, nd, fan_in), BF16),
            pltpu.VMEM((C - 1, nd, fan_in), BF16),
            pltpu.VMEM((R * nd, classes), BF16),
            pltpu.VMEM((C - 1, nd, classes), BF16),
            pltpu.VMEM((C - 1, nd, classes), BF16),
            pltpu.VMEM((C, nd + LOSS_ROWS, classes), BF16),
            pltpu.VMEM((R - 1, nd + LOSS_ROWS, classes), BF16),
            pltpu.VMEM((R, nd + LOSS_ROWS, classes), BF16),
            pltpu.VMEM((grad_rows, TILE), BF16),
            pltpu.VMEM((C - 1, chunk, TILE), BF16),
            pltpu.VMEM((R, chunk, TILE), BF16),
            pltpu.VMEM((grad_rows, TILE), BF16),
            pltpu.SemaphoreType.DMA((10, most)),
            pltpu.SemaphoreType.DMA((10, most)),
        ],
        compiler_params=pltpu.CompilerParams(
            collective_id=0, has_side_effects=True, vmem_limit_bytes=VMEM_LIMIT
        ),
        name="train_step",
    )(adjacency, features, norm_weight[None, :], weight_in, weight_out, labels[None, :])
    return grad_in, grad_out, loss[0, 0]


def solution(mesh):
    in_specs = (
        P(("row", "col"), None),
        P(("row", "col")),
        P(),
        P(),
        P(("row", "col")),
        P(("row", "col"), None),
        P(("row", "col"), None, None, None),
        P(("row", "col")),
    )
    out_specs = (P(), P(), P())
    return jax.shard_map(
        per_device, mesh=mesh, in_specs=in_specs, out_specs=out_specs, check_vma=False
    )
```

```python
import functools

import jax
import jax.numpy as jnp
from jax import lax
from jax.experimental import pallas as pl
from jax.experimental.pallas import tpu as pltpu
from jax.sharding import PartitionSpec as P

TILE = 128
SOFTCAP = 15.0
LOSS_SCALE = 1024.0
UNROLL = 32
LOSS_ROWS = 16
MESH = pl.DeviceIdType.MESH
F32 = jnp.float32
BF16 = jnp.bfloat16
VMEM_LIMIT = 56 * 1024 * 1024


def dot(a, b, ca=1, cb=0):
    return lax.dot_general(a, b, (((ca,), (cb,)), ((), ())), preferred_element_type=F32)


def split2(x):
    hi = x.astype(BF16)
    return hi, (x - hi.astype(F32)).astype(BF16)


def densify_kernel(row_tiles, col_tiles, count_ref, slot_ref, edges_ref, out_ref, acc):
    places = row_tiles * col_tiles
    count = count_ref[0]
    acc[...] = jnp.zeros_like(acc)
    entries = edges_ref.shape[3]
    iota = lax.broadcasted_iota(jnp.int32, (TILE, entries), 0).astype(F32).astype(BF16)
    ones, zeros = jnp.ones(iota.shape, BF16), jnp.zeros(iota.shape, BF16)

    def body(step, carry):
        found = []
        for u in range(UNROLL):
            s = step * UNROLL + u
            edges = edges_ref[0, s].astype(F32).astype(BF16)
            rows = jnp.where(iota == edges[0:1, :], ones, zeros)
            cols = jnp.where(iota == edges[1:2, :], ones, zeros)
            found.append((jnp.where(s < count, slot_ref[0, s], places), dot(rows, cols, 1, 1)))
        for p, tile in found:
            acc[p] += tile
        return carry

    lax.fori_loop(0, (count + UNROLL - 1) // UNROLL, body, 0)
    for r in range(row_tiles):
        for c in range(col_tiles):
            out_ref[r * TILE : (r + 1) * TILE, c * TILE : (c + 1) * TILE] = acc[
                r * col_tiles + c
            ].astype(BF16)


def densify(tile_slot, tile_edges, tile_count, row_group, col_group):
    row_tiles, col_tiles = row_group // TILE, col_group // TILE
    return pl.pallas_call(
        functools.partial(densify_kernel, row_tiles, col_tiles),
        out_shape=jax.ShapeDtypeStruct((row_group, col_group), BF16),
        in_specs=[
            pl.BlockSpec(memory_space=pltpu.SMEM),
            pl.BlockSpec(memory_space=pltpu.SMEM),
            pl.BlockSpec(memory_space=pltpu.VMEM),
        ],
        out_specs=pl.BlockSpec(memory_space=pltpu.VMEM),
        scratch_shapes=[pltpu.VMEM((row_tiles * col_tiles + 1, TILE, TILE), F32)],
        compiler_params=pltpu.CompilerParams(vmem_limit_bytes=VMEM_LIMIT),
        name="densify",
    )(tile_count, tile_slot, tile_edges)


def step_kernel(
    R, C, nd, adj, feat, norm, w_in, w_out, labels,
    grad_in, grad_out, loss_out,
    gath_one, part_one, recv_one, part_low, recv_low, gath_two, part_two, recv_two,
    gath_back, part_back, recv_back, part_grad, recv_grad, slots_grad, full_grad,
    send_sem, recv_sem, *direct_refs,
):
    i = lax.axis_index("row")
    j = lax.axis_index("col")
    total_nodes = nd * R * C
    pending = []

    def row_peer(k):
        return (lax.rem(i + k, R), j)

    def col_peer(k):
        return (i, lax.rem(j + k, C))

    def send(phase, k, peer, src, dst):
        copy = pltpu.make_async_remote_copy(
            src_ref=src, dst_ref=dst,
            send_sem=send_sem.at[phase, k - 1], recv_sem=recv_sem.at[phase, k - 1],
            device_id=peer, device_id_type=MESH,
        )
        copy.start()
        pending.append(copy)
        return copy

    def arrive(copies):
        for copy in copies:
            copy.wait_recv()

    barrier = pltpu.get_barrier_semaphore()
    greeted = [row_peer(k) for k in range(1, R)] + [col_peer(k) for k in range(1, C)]
    others = [(a, b) for a in range(R) for b in range(C) if a + b > 0]
    if direct_refs:
        greeted = [(lax.rem(i + a, R), lax.rem(j + b, C)) for a, b in others]
    for peer in greeted:
        pl.semaphore_signal(barrier, inc=1, device_id=peer, device_id_type=MESH)

    scale = jnp.transpose(jnp.broadcast_to(norm[...], (nd, nd)))
    normed = (scale * feat[...].astype(F32)).astype(BF16)
    mine = pl.ds(pl.multiple_of(i * nd, nd), nd)
    gath_one[mine, :] = normed
    pl.semaphore_wait(barrier, len(greeted))

    def block_of(t):
        return adj[pl.ds(pl.multiple_of(t * nd, nd), nd), :]

    arrive([send(0, k, row_peer(k), gath_one.at[mine], gath_one.at[mine]) for k in range(1, R)])
    values = gath_one[...]
    copies = []
    for k in range(1, C):
        part_one[k - 1], part_low[k - 1] = split2(dot(block_of(lax.rem(j + k, C)), values))
        copies.append(send(1, k, col_peer(k), part_one.at[k - 1], recv_one.at[k - 1]))
    low_copies = [
        send(9, k, col_peer(k), part_low.at[k - 1], recv_low.at[k - 1]) for k in range(1, C)
    ]
    mixed = dot(block_of(j), values) + normed.astype(F32)
    for k in range(1, C):
        copies[k - 1].wait_recv()
        mixed = mixed + recv_one[k - 1].astype(F32)
    w = w_in[...]
    scale_wide = jnp.concatenate([scale, scale], axis=1)
    m_hi, m_lo = split2(mixed)
    hidden_ahead = jnp.maximum(scale_wide * (dot(m_hi, w) + dot(m_lo, w)), 0.0).astype(BF16)
    source_two = (scale * dot(hidden_ahead, w_out[...])).astype(BF16)
    gath_two[mine, :] = source_two
    arrive([send(2, k, row_peer(k), gath_two.at[mine], gath_two.at[mine]) for k in range(1, R)])
    values = gath_two[...]
    copies = []
    for k in range(1, C):
        part_two[k - 1] = dot(block_of(lax.rem(j + k, C)), values).astype(BF16)
        copies.append(send(3, k, col_peer(k), part_two.at[k - 1], recv_two.at[k - 1]))
    logits = dot(block_of(j), values) + source_two.astype(F32)
    for k in range(1, C):
        copies[k - 1].wait_recv()
        logits = logits + recv_two[k - 1].astype(F32)
    logits = scale * logits
    ratio = jnp.tanh(logits * (1.0 / SOFTCAP))
    capped = SOFTCAP * ratio
    exp_capped = jnp.exp(capped)
    exp_total = jnp.sum(exp_capped, axis=1, keepdims=True)
    label_rows = jnp.transpose(jnp.broadcast_to(labels[...].astype(F32), (nd, nd)))
    one_hot = jnp.where(
        label_rows == lax.broadcasted_iota(jnp.int32, (nd, nd), 1).astype(F32), 1.0, 0.0
    )
    node_loss = jnp.log(exp_total) - jnp.sum(capped * one_hot, axis=1, keepdims=True)
    loss_local = jnp.sum(node_loss, axis=0, keepdims=True)
    d_logits = (LOSS_SCALE / total_nodes) * (exp_capped / exp_total - one_hot) * (
        1.0 - ratio * ratio
    )
    back_two = (scale * d_logits).astype(BF16)

    upper = lax.broadcasted_iota(jnp.int32, (LOSS_ROWS, TILE), 0) < LOSS_ROWS // 2

    def loss_rows(value):
        value = jnp.broadcast_to(value, (LOSS_ROWS, TILE))
        hi, lo = split2(value)
        return jnp.where(upper, hi.astype(F32), lo.astype(F32)).astype(BF16)

    def read_loss(rows):
        rows = rows.astype(F32)
        return rows[0:1, :] + rows[LOSS_ROWS // 2 : LOSS_ROWS // 2 + 1, :]

    gath_back[j, :nd, :] = jnp.transpose(back_two.astype(F32)).astype(BF16)
    gath_back[j, nd:, :] = loss_rows(loss_local)
    copies = [send(4, k, col_peer(k), gath_back.at[j], gath_back.at[j]) for k in range(1, C)]
    arrive(low_copies)
    low = recv_low[0].astype(F32)
    for k in range(2, C):
        low = low + recv_low[k - 1].astype(F32)
    mixed = mixed + low
    m_hi, m_lo = split2(mixed)
    m_least = (mixed - m_hi.astype(F32) - m_lo.astype(F32)).astype(BF16)
    pre_hidden = scale_wide * (dot(m_hi, w) + (dot(m_lo, w) + dot(m_least, w)))
    hidden = jnp.maximum(pre_hidden, 0.0).astype(BF16)
    arrive(copies)
    loss_col = read_loss(gath_back[0, nd:, :])
    for k in range(1, C):
        loss_col = loss_col + read_loss(gath_back[k, nd:, :])
    values_t = jnp.concatenate([gath_back[k, :nd, :] for k in range(C)], axis=1)
    rows_loss = loss_rows(loss_col)

    def back_of(t):
        return dot(values_t, adj[:, pl.ds(pl.multiple_of(t * nd, nd), nd)])

    copies = []
    for k in range(1, R):
        part_back[k - 1, :nd, :] = back_of(lax.rem(i + k, R)).astype(BF16)
        part_back[k - 1, nd:, :] = rows_loss
        copies.append(send(5, k, row_peer(k), part_back.at[k - 1], recv_back.at[i]))
    recv_back[i, nd:, :] = rows_loss
    summed = back_of(i)
    arrive(copies)
    recv_back[i, :nd, :] = jnp.zeros((nd, nd), BF16)
    loss_all = read_loss(recv_back[0, nd:, :])
    for k in range(1, R):
        loss_all = loss_all + read_loss(recv_back[k, nd:, :])
    for k in range(R):
        summed = summed + recv_back[k, :nd, :].astype(F32)
    loss_out[...] = jnp.broadcast_to(loss_all * (1.0 / total_nodes), loss_out.shape)
    d_source = scale * (jnp.transpose(summed) + back_two.astype(F32))
    d_hi, d_lo = split2(d_source)
    d_hidden = dot(d_hi, w_out[...], 1, 1) + dot(d_lo, w_out[...], 1, 1)
    back_one = jnp.where(
        pre_hidden > 0, scale_wide * d_hidden, 0.0
    ).astype(BF16)
    local_out = dot(hidden, d_hi, 0, 0) + dot(hidden, d_lo, 0, 0)
    local_in = dot(m_hi, back_one, 0, 0) + dot(m_lo, back_one, 0, 0)

    fan_in, half = local_in.shape[0], TILE
    hid = local_in.shape[1]
    for h in range(hid // half):
        part_grad[h * fan_in : (h + 1) * fan_in, :] = local_in[:, h * half : (h + 1) * half].astype(
            BF16
        )
    base = fan_in * (hid // half)
    part_grad[base:, :] = local_out.astype(BF16)

    chunk = full_grad.shape[0] // (R * C if direct_refs else C)

    def rows_of(t):
        return pl.ds(pl.multiple_of(t * chunk, chunk), chunk)

    if direct_refs:
        recv_all, send_all, sem_all = direct_refs

        def send_to(phase, q, src, dst):
            a, b = others[q]
            copy = pltpu.make_async_remote_copy(
                src_ref=src, dst_ref=dst,
                send_sem=send_all.at[phase, q], recv_sem=sem_all.at[phase, q],
                device_id=(lax.rem(i + a, R), lax.rem(j + b, C)), device_id_type=MESH,
            )
            copy.start()
            pending.append(copy)
            return copy

        copies = []
        for q, (a, b) in enumerate(others):
            owner = lax.rem(i + a, R) * C + lax.rem(j + b, C)
            copies.append(send_to(0, q, part_grad.at[rows_of(owner)], recv_all.at[q]))
        own = rows_of(i * C + j)
        total = part_grad[own, :].astype(F32)
        for q in range(len(others)):
            copies[q].wait_recv()
            total = total + recv_all[q].astype(F32)
        full_grad[own, :] = total.astype(BF16)
        arrive(
            [send_to(1, q, full_grad.at[own], full_grad.at[own]) for q in range(len(others))]
        )
    else:
        copies = [
            send(6, k, col_peer(k), part_grad.at[rows_of(lax.rem(j + k, C))], recv_grad.at[k - 1])
            for k in range(1, C)
        ]
        total = part_grad[rows_of(j), :].astype(F32)
        for k in range(1, C):
            copies[k - 1].wait_recv()
            total = total + recv_grad[k - 1].astype(F32)
        slots_grad[i] = total.astype(BF16)
        arrive([send(7, k, row_peer(k), slots_grad.at[i], slots_grad.at[i]) for k in range(1, R)])
        total = slots_grad[0].astype(F32)
        for k in range(1, R):
            total = total + slots_grad[k].astype(F32)
        full_grad[rows_of(j), :] = total.astype(BF16)
        arrive(
            [
                send(8, k, col_peer(k), full_grad.at[rows_of(j)], full_grad.at[rows_of(j)])
                for k in range(1, C)
            ]
        )
    for h in range(hid // half):
        grad_in[:, h * half : (h + 1) * half] = full_grad[h * fan_in : (h + 1) * fan_in, :].astype(
            F32
        )
    grad_out[...] = full_grad[base:, :].astype(F32)
    for copy in pending:
        copy.wait_send()


def per_device(
    features, norm_weight, weight_in, weight_out, labels, tile_slot, tile_edges, tile_count
):
    R = lax.axis_size("row")
    C = lax.axis_size("col")
    nd, fan_in = features.shape
    hid, classes = weight_out.shape
    adjacency = densify(tile_slot, tile_edges, tile_count, nd * C, nd * R)
    grad_rows = (fan_in * hid + hid * classes) // TILE
    chunk = grad_rows // C
    most = max(R, C) - 1
    direct = []
    if grad_rows % (R * C * 16) == 0:
        direct = [
            pltpu.VMEM((R * C - 1, grad_rows // (R * C), TILE), BF16),
            pltpu.SemaphoreType.DMA((2, R * C - 1)),
            pltpu.SemaphoreType.DMA((2, R * C - 1)),
        ]
    vmem = pl.BlockSpec(memory_space=pltpu.VMEM)
    grad_in, grad_out, loss = pl.pallas_call(
        functools.partial(step_kernel, R, C, nd),
        out_shape=(
            jax.ShapeDtypeStruct((fan_in, hid), F32),
            jax.ShapeDtypeStruct((hid, classes), F32),
            jax.ShapeDtypeStruct((1, TILE), F32),
        ),
        in_specs=[vmem] * 6,
        out_specs=(vmem, vmem, vmem),
        scratch_shapes=[
            pltpu.VMEM((R * nd, fan_in), BF16),
            pltpu.VMEM((C - 1, nd, fan_in), BF16),
            pltpu.VMEM((C - 1, nd, fan_in), BF16),
            pltpu.VMEM((C - 1, nd, fan_in), BF16),
            pltpu.VMEM((C - 1, nd, fan_in), BF16),
            pltpu.VMEM((R * nd, classes), BF16),
            pltpu.VMEM((C - 1, nd, classes), BF16),
            pltpu.VMEM((C - 1, nd, classes), BF16),
            pltpu.VMEM((C, nd + LOSS_ROWS, classes), BF16),
            pltpu.VMEM((R - 1, nd + LOSS_ROWS, classes), BF16),
            pltpu.VMEM((R, nd + LOSS_ROWS, classes), BF16),
            pltpu.VMEM((grad_rows, TILE), BF16),
            pltpu.VMEM((C - 1, chunk, TILE), BF16),
            pltpu.VMEM((R, chunk, TILE), BF16),
            pltpu.VMEM((grad_rows, TILE), BF16),
            pltpu.SemaphoreType.DMA((10, most)),
            pltpu.SemaphoreType.DMA((10, most)),
            *direct,
        ],
        compiler_params=pltpu.CompilerParams(
            collective_id=0, has_side_effects=True, vmem_limit_bytes=VMEM_LIMIT
        ),
        name="train_step",
    )(adjacency, features, norm_weight[None, :], weight_in, weight_out, labels[None, :])
    return grad_in, grad_out, loss[0, 0]


def solution(mesh):
    in_specs = (
        P(("row", "col"), None),
        P(("row", "col")),
        P(),
        P(),
        P(("row", "col")),
        P(("row", "col"), None),
        P(("row", "col"), None, None, None),
        P(("row", "col")),
    )
    out_specs = (P(), P(), P())
    return jax.shard_map(
        per_device, mesh=mesh, in_specs=in_specs, out_specs=out_specs, check_vma=False
    )
```
